32 devices in a mesh: expert: 4 (over y, x), dp: 8 (over z, core).
Axes of the slice: x: 2, y: 2, z: 4, core: 2. Of those that a mesh axis runs over, the one named last changes fastest.
Arguments:
- tokens: bfloat16 [256, 4096], P(('expert', 'dp')), may hold values from -6 to 6
- routes: int32 [256, 2], P(('expert', 'dp')), may hold values from 0 to 3, all different within a row; in each aligned block of 8 rows (0 to 7, 8 to 15, ...) at most 6 rows name the same one
- route_weights: float32 [256, 2], P(('expert', 'dp')), may hold values from 0.2 to 1
- w_gate: bfloat16 [4, 4096, 14336], P('expert', None, 'dp'), may hold values from -0.09375 to 0.09375
- w_up: bfloat16 [4, 4096, 14336], P('expert', None, 'dp'), may hold values from -0.09375 to 0.09375
- w_down: bfloat16 [4, 14336, 4096], P('expert', 'dp'), may hold values from -0.046875 to 0.046875
Outputs:
- mixed: bfloat16 [256, 4096], P(('expert', 'dp'))
The draws below stay inside these ranges and needn't reach their ends.
Inputs may be any that keep to these rules, and one draw needn't show every extreme that they name: `routes`: within the rows of one device (aligned blocks of 8 rows) the two experts of a token differ and no expert is named more than 6 times; in every draw some block names some expert exactly 6 times. Every expert is named somewhere.
All inputs are finite; a program needn't handle non-finite values.
Results may differ from the reference program's by a relative error of at most 0.0057.
Values may be sent and summed in bfloat16 or wider, within the bound.
A program may use at most 128 MiB of HBM per device.

```python
import math
import jax
import jax.numpy as jnp
import numpy as np
from jax import lax

D = 4096
FF = 14336
TOK_DEV = 8
EXPERTS = 4
CAP = 6
TOKENS = 256
N_EXPERT = 4
N_DP = 8


def levels(own_key, extent, cuts, low, top_value):
    loudness, own = 1.0, jax.random.fold_in(own_key, 6)
    for axis_at, blocks in cuts:
        steps = jnp.exp(jax.random.uniform(jax.random.fold_in(own, axis_at), (blocks,), jnp.float32, low / len(cuts), top_value / len(cuts)))
        loudness = loudness * jnp.repeat(steps, extent[axis_at] // blocks).reshape([-1 if axis == axis_at else 1 for axis in range(len(extent))])
    return loudness


def routed_block(key, own, number, rows, count, top, limit, skew):
    order = jax.random.permutation(key, count)
    heavy_load, common = shares(count, rows * top, limit, skew, True), shares(count, rows * top, limit, skew, False)
    places = jnp.arange(count)

    def named(lengths, rotation):
        used = int((lengths > 0).sum())
        fixed = max(1, used // 4)
        moved = fixed + (places - fixed + rotation * (used - fixed)) % max(1, count - fixed)
        return jnp.zeros((count,), jnp.int32).at[order[jnp.where(places < fixed, places, moved)]].set(jnp.asarray(lengths, jnp.int32))

    lengths = jnp.where(number % 4 == 0, named(heavy_load, number // 4), named(common, number - number // 4 - 1))
    mixed = jax.random.permutation(jax.random.fold_in(own, 3), count)
    giver, sink = mixed[0:count // 2 * 2:2], mixed[1:count // 2 * 2:2]
    room = jnp.minimum(lengths[giver] - 1, limit - lengths[sink]) // 2
    room = jnp.where((giver == order[0]) | (sink == order[0]) | (lengths[sink] == 0), 0, jnp.maximum(room, 0))
    moved = jax.random.randint(jax.random.fold_in(own, 4), (count // 2,), 0, 1 << 20) % (room + 1)
    lengths = lengths.at[giver].add(-moved).at[sink].add(moved)
    items = jnp.searchsorted(jnp.cumsum(lengths), jnp.arange(rows * top), side="right").astype(jnp.int32)
    table = items.reshape(top, rows).T
    table = table[jax.random.permutation(jax.random.fold_in(own, 1), rows)]
    rotation = jax.random.randint(jax.random.fold_in(own, 2), (rows, 1), 0, top)
    return jnp.take_along_axis(table, (jnp.arange(top)[None, :] + rotation) % top, axis=1)


def shares(amount, total, reach, slope, full):
    weights = [(1 << 20) // math.isqrt(rank ** slope) + 1 for rank in range(1, amount + 1)]
    largest = reach if full else min(reach, max(-(-total // amount), total * weights[0] // sum(weights)))
    least = 1 if total - largest >= amount - 1 else 0
    counts, rest = [largest] + [least] * (amount - 1), total - largest - least * (amount - 1)
    while rest > 0:
        candidates = [i for i in range(1, amount) if counts[i] < largest] or [i for i in range(1, amount) if counts[i] < reach]
        whole, remaining = sum([weights[i] for i in candidates]), rest
        for i in candidates:
            addition = min(reach - counts[i], max(1, remaining * weights[i] // whole), rest)
            counts[i] = counts[i] + addition
            rest = rest - addition
    return np.array(counts)


def centred(own_key, shape, spread, most, cuts=(), kind=jnp.bfloat16):
    factor_of = levels(own_key, shape, cuts, -0.22, 0.18) if cuts else 1.0
    values = jax.random.normal(own_key, shape, jnp.float32) * spread * factor_of
    return jnp.minimum(jnp.maximum(values, -most), most).astype(kind)


def setup_inputs(seed: int = 0) -> dict:
    keys = jax.random.split(jax.random.key(seed), 7)
    tokens = centred(keys[0], (TOKENS, D), 1.0, 6.0, ((0, 32),))
    routes_keys = jax.random.split(jax.random.fold_in(keys[1], 1), TOKENS // TOK_DEV)
    routes_turns = jax.random.permutation(jax.random.fold_in(keys[1], 3), TOKENS // TOK_DEV)
    routes = jax.vmap(lambda own, number: routed_block(jax.random.fold_in(keys[1], 2), own, number, TOK_DEV, EXPERTS, 2, CAP, 2))(routes_keys, routes_turns).reshape((TOKENS, 2))
    route_weights = jnp.clip(0.2 + 0.8 * jax.random.uniform(keys[2], (TOKENS, 2), jnp.float32) ** levels(keys[2], (TOKENS, 2), ((0, 32),), -0.2, 0.2), 0.2, 1.0)
    w_gate = centred(keys[3], (EXPERTS, D, FF), D ** -0.5, 0.09375, ((0, 4), (2, 8)))
    w_up = centred(keys[4], (EXPERTS, D, FF), D ** -0.5, 0.09375, ((0, 4), (2, 8)))
    w_down = centred(keys[5], (EXPERTS, FF, D), FF ** -0.5, 0.046875, ((0, 4), (1, 8)))
    return dict(tokens=tokens, routes=routes, route_weights=route_weights, w_gate=w_gate, w_up=w_up, w_down=w_down)


def slot_columns(routes):
    devices = N_EXPERT * N_DP
    listed = routes.reshape(devices, TOK_DEV * 2)
    chosen = (listed[:, :, None] == jnp.arange(EXPERTS, dtype=jnp.int32)[None, None, :]).astype(jnp.int32)
    before = jnp.cumsum(chosen, axis=1) - chosen
    return listed * CAP + jnp.sum(before * chosen, axis=2)


def reference(tokens, routes, route_weights, w_gate, w_up, w_down):
    devices = N_EXPERT * N_DP
    columns = EXPERTS * CAP
    slice_units = FF // N_DP
    column = slot_columns(routes)
    placing = (column[:, :, None] == jnp.arange(columns, dtype=jnp.int32)[None, None, :]).astype(jnp.float32)
    placing = placing.reshape(devices, TOK_DEV, 2, columns)
    sending = jnp.sum(placing, axis=2)
    token_blocks = tokens.reshape(devices, TOK_DEV, D).astype(jnp.float32)
    outgoing = jnp.einsum("ntw,ntd->nwd", sending, token_blocks).astype(jnp.bfloat16)
    expert_rows = outgoing.reshape(devices, EXPERTS, CAP, D).transpose(1, 0, 2, 3).reshape(EXPERTS, devices * CAP, D)

    def one_expert(operands):
        inputs, gate_full, up_full, down_full = operands
        gate_slices = gate_full.reshape(D, N_DP, slice_units).transpose(1, 0, 2)
        up_slices = up_full.reshape(D, N_DP, slice_units).transpose(1, 0, 2)
        down_slices = down_full.reshape(N_DP, slice_units, D)

        def add_slice(total, pieces):
            gate_piece, up_piece, down_piece = pieces
            gated = jnp.dot(inputs, gate_piece, preferred_element_type=jnp.float32)
            upward = jnp.dot(inputs, up_piece, preferred_element_type=jnp.float32)
            hidden = (jax.nn.silu(gated) * upward).astype(jnp.bfloat16)
            part = jnp.dot(hidden, down_piece, preferred_element_type=jnp.float32)
            return total + part, None

        start_total = jnp.zeros((inputs.shape[0], D), jnp.float32)
        total, unused = lax.scan(add_slice, start_total, (gate_slices, up_slices, down_slices))
        return total.astype(jnp.bfloat16)

    expert_out = lax.map(one_expert, (expert_rows, w_gate, w_up, w_down))
    returned = expert_out.reshape(EXPERTS, devices, CAP, D).transpose(1, 0, 2, 3).reshape(devices, columns, D)
    picked = jnp.einsum("ntkw,nwd->ntkd", placing, returned.astype(jnp.float32))
    weights = route_weights.reshape(devices, TOK_DEV, 2)
    mixed = jnp.sum(weights[:, :, :, None] * picked, axis=2)
    return mixed.reshape(TOKENS, D).astype(jnp.bfloat16)
```

```python
import functools

import jax
import jax.numpy as jnp
from jax import lax
from jax.experimental import pallas as pl
from jax.experimental.pallas import tpu as pltpu
from jax.sharding import PartitionSpec as P

MESH = pl.DeviceIdType.MESH
BF16 = jnp.bfloat16
F32 = jnp.float32
CHUNKS = 2


def tile_of(extent, most):
    return max([t for t in range(128, most + 1, 128) if extent % t == 0], default=extent)


def kernel(
    groups, ranks, capacity, block,
    tokens, routes, weights, gate_hbm, up_hbm, down_hbm, out,
    gate, up, down, w_sem,
    pair_send, pair_recv, meta, gathered,
    chosen_rows, lhs, g_acc, u_acc, hidden,
    half_send, half_recv, summed, returned, mixed_send, mixed_recv, last_send, last_recv,
    a_sem, b_sem, bm_sem, c_sem, d_sem, e_sem, f_sem, g_sem, h_sem,
):
    expert = lax.axis_index("expert")
    rank = lax.axis_index("dp")
    chips = ranks // 2
    chip, core = rank // 2, lax.rem(rank, 2)
    twin = chip * 2 + (1 - core)
    count, features = tokens.shape
    units = gate_hbm.shape[1]
    half = features // 2
    width = half // CHUNKS
    rows = groups * block
    both = 2 * count
    own_tokens = pl.ds(pl.multiple_of(chip * both, both), both)
    own_rows = pl.ds(pl.multiple_of(expert * block, block), block)

    def remote(src, dst, sems, index, where):
        return pltpu.make_async_remote_copy(
            src_ref=src, dst_ref=dst, send_sem=sems.at[(0, *index)], recv_sem=sems.at[(1, *index)],
            device_id=where, device_id_type=MESH,
        )

    to_twin = {"dp": twin}
    chip_peers = [(d, {"dp": lax.rem(chip + d, chips) * 2 + core}, lax.rem(chip + d, chips)) for d in range(1, chips)]
    expert_peers = [(d, {"expert": lax.rem(expert + d, groups)}, lax.rem(expert + d, groups)) for d in range(1, groups)]

    loads = {}
    for q in range(CHUNKS):
        for side in range(2):
            at = (core if side == 0 else 1 - core) * CHUNKS + q
            span = pl.ds(pl.multiple_of(at * width, width), width)
            loads["in", q, side] = (
                pltpu.make_async_copy(gate_hbm.at[span, :], gate.at[at], w_sem.at[0, q, side]),
                pltpu.make_async_copy(up_hbm.at[span, :], up.at[at], w_sem.at[1, q, side]),
            )
            for copy in loads["in", q, side]:
                copy.start()
    for q in range(CHUNKS):
        for side in (1, 0):
            at = (core if side == 0 else 1 - core) * CHUNKS + q
            span = pl.ds(pl.multiple_of(at * width, width), width)
            loads["out", q, side] = (pltpu.make_async_copy(down_hbm.at[:, span], down.at[at], w_sem.at[2, q, side]),)
            loads["out", q, side][0].start()

    barrier = pltpu.get_barrier_semaphore()
    pl.semaphore_signal(barrier, inc=1, device_id=to_twin, device_id_type=MESH)
    for _, where, _ in chip_peers + expert_peers:
        pl.semaphore_signal(barrier, inc=1, device_id=where, device_id_type=MESH)

    lanes = lax.broadcasted_iota(jnp.int32, (count, 128), 1)
    first, second = routes[:, 0:1], routes[:, 1:2]
    is_first = (lanes == first).astype(F32)
    is_second = (lanes == second).astype(F32)
    earlier = (
        lax.broadcasted_iota(jnp.int32, (count, count), 1) < lax.broadcasted_iota(jnp.int32, (count, count), 0)
    ).astype(F32)
    before = jnp.dot(earlier, is_first + is_second, preferred_element_type=F32)
    slot_first = jnp.sum(before * is_first, axis=1, keepdims=True)
    slot_second = jnp.sum((before + is_first) * is_second, axis=1, keepdims=True)
    base = (rank * capacity).astype(F32)
    row_first = first.astype(F32) * block + base + slot_first
    row_second = second.astype(F32) * block + base + slot_second
    facts = jnp.where(lanes == 0, row_first, 0.0)
    facts = jnp.where(lanes == 1, row_second, facts)
    facts = jnp.where(lanes == 2, weights[:, 0:1], facts)
    facts = jnp.where(lanes == 3, weights[:, 1:2], facts)
    own_facts = meta.at[pl.ds(pl.multiple_of(rank * count, count), count), :]
    own_facts[...] = facts

    everything = tokens[...].astype(F32)
    left, right = everything[:, :half], everything[:, half:]
    mine = jnp.where(core == 0, left, right)
    other = jnp.where(core == 0, right, left)
    pair_send[...] = jnp.concatenate([other[:, : half // 2], other[:, half // 2 :]], axis=0).astype(BF16)

    pl.semaphore_wait(barrier, 1 + len(chip_peers) + len(expert_peers))

    a_rows = remote(pair_send, pair_recv, a_sem, (0,), to_twin)
    a_meta = remote(own_facts, own_facts, a_sem, (1,), to_twin)
    a_rows.start()
    a_meta.start()
    a_rows.wait_recv()
    a_meta.wait_recv()
    got = pair_recv[...].astype(F32)
    theirs = jnp.concatenate([got[:count], got[count:]], axis=1)
    sixteen = jnp.concatenate(
        [jnp.where(core == 0, mine, theirs), jnp.where(core == 0, theirs, mine)], axis=0
    ).astype(BF16)

    b_copies, bm_copies = {}, []
    for d, where, _ in chip_peers:
        part = meta.at[own_tokens, :]
        bm_copies.append(remote(part, part, bm_sem, (d - 1,), where))
        bm_copies[-1].start()
    for q in range(CHUNKS):
        gathered[q, own_tokens, :] = sixteen[:, q * width : (q + 1) * width]
        for d, where, _ in chip_peers:
            part = gathered.at[q, own_tokens, :]
            b_copies[q, d] = remote(part, part, b_sem, (q, d - 1), where)
            b_copies[q, d].start()
    for copy in bm_copies:
        copy.wait_recv()
    table = meta[...]
    row_ids = lax.broadcasted_iota(jnp.int32, (ranks * count, rows), 1).astype(F32)
    pick_first = (row_ids == table[:, 0:1]).astype(BF16)
    pick_second = (row_ids == table[:, 1:2]).astype(BF16)
    picks = jnp.concatenate([pick_first, pick_second], axis=0)
    placing = pick_first + pick_second

    c_copies, d_copies = {}, {}
    for q in range(CHUNKS):
        for d, _, _ in chip_peers:
            b_copies[q, d].wait_recv()
        chosen_rows[q] = lax.dot_general(
            placing, gathered[q], (((0,), (0,)), ((), ())), preferred_element_type=F32
        ).astype(BF16)
        for d, where, there in expert_peers:
            c_copies[q, d] = remote(
                chosen_rows.at[q, pl.ds(pl.multiple_of(there * block, block), block), :],
                lhs.at[core, q, own_rows, :], c_sem, (q, d - 1), where,
            )
            c_copies[q, d].start()
        lhs[core, q, own_rows, :] = chosen_rows[q, own_rows, :]
        part = lhs.at[core, q, own_rows, :]
        d_copies[q, 0] = remote(part, part, d_sem, (q, 0), to_twin)
        d_copies[q, 0].start()

    unit_tile = tile_of(units, 512)

    def accumulate(q, side, fresh):
        at = core if side == 0 else 1 - core
        for copy in loads["in", q, side]:
            copy.wait()
        piece = at * CHUNKS + q

        def step(n, carry):
            span = pl.ds(pl.multiple_of(n * unit_tile, unit_tile), unit_tile)
            x = lhs[at, q]
            g = jnp.dot(x, gate[piece, :, span], preferred_element_type=F32)
            u = jnp.dot(x, up[piece, :, span], preferred_element_type=F32)
            if fresh:
                g_acc[:, span] = g
                u_acc[:, span] = u
            else:
                g_acc[:, span] += g
                u_acc[:, span] += u
            return carry

        lax.fori_loop(0, units // unit_tile, step, 0)

    for q in range(CHUNKS):
        for d, _, _ in expert_peers:
            c_copies[q, d].wait_recv()
            source = lax.rem(expert + groups - d, groups)
            part = lhs.at[core, q, pl.ds(pl.multiple_of(source * block, block), block), :]
            d_copies[q, d] = remote(part, part, d_sem, (q, d), to_twin)
            d_copies[q, d].start()
        accumulate(q, 0, q == 0)
        for d in range(groups):
            d_copies[q, d].wait_recv()
        accumulate(q, 1, False)

    def activate(n, carry):
        span = pl.ds(pl.multiple_of(n * unit_tile, unit_tile), unit_tile)
        g = g_acc[:, span]
        hidden[:, span] = (g / (1.0 + jnp.exp(-g)) * u_acc[:, span]).astype(BF16)
        return carry

    lax.fori_loop(0, units // unit_tile, activate, 0)

    out_tile = tile_of(width, 512)
    e_copies, f_copies = {}, {}
    for q in range(CHUNKS):
        loads["out", q, 1][0].wait()

        def foreign(n, carry):
            span = pl.ds(pl.multiple_of(n * out_tile, out_tile), out_tile)
            half_send[q, :, span] = jnp.dot(
                hidden[...], down[(1 - core) * CHUNKS + q, :, span], preferred_element_type=F32
            ).astype(BF16)
            return carry

        lax.fori_loop(0, width // out_tile, foreign, 0)
        e_copies[q] = remote(half_send.at[q], half_recv.at[q], e_sem, (q,), to_twin)
        e_copies[q].start()
        loads["out", q, 0][0].wait()
        e_copies[q].wait_recv()

        def native(n, carry):
            span = pl.ds(pl.multiple_of(n * out_tile, out_tile), out_tile)
            part = jnp.dot(hidden[...], down[core * CHUNKS + q, :, span], preferred_element_type=F32)
            summed[q, :, span] = (part + half_recv[q, :, span].astype(F32)).astype(BF16)
            return carry

        lax.fori_loop(0, width // out_tile, native, 0)
        for d, where, there in expert_peers:
            f_copies[q, d] = remote(
                summed.at[q, pl.ds(pl.multiple_of(there * block, block), block), :],
                returned.at[q, own_rows, :], f_sem, (q, d - 1), where,
            )
            f_copies[q, d].start()
        returned[q, own_rows, :] = summed[q, own_rows, :]

    g_copies = {}
    for q in range(CHUNKS):
        for d, _, _ in expert_peers:
            f_copies[q, d].wait_recv()
        picked = jnp.dot(picks, returned[q], preferred_element_type=F32)
        half_count = ranks * count
        mixture = table[:, 2:3] * picked[:half_count] + table[:, 3:4] * picked[half_count:]
        mixed_send[q] = mixture.astype(BF16)
        for d, where, there in chip_peers:
            g_copies[q, d] = remote(
                mixed_send.at[q, pl.ds(pl.multiple_of(there * both, both), both), :],
                mixed_recv.at[q, own_tokens, :], g_sem, (q, d - 1), where,
            )
            g_copies[q, d].start()
        mixed_recv[q, own_tokens, :] = mixed_send[q, own_tokens, :]

    h_copies = {}
    for q in range(CHUNKS):
        for d, _, _ in chip_peers:
            g_copies[q, d].wait_recv()
        total = mixed_recv[q, 0:both, :].astype(F32)
        for z in range(1, chips):
            total = total + mixed_recv[q, z * both : (z + 1) * both, :].astype(F32)
        low, high = total[:count], total[count:]
        keep = jnp.where(core == 0, low, high)
        give = jnp.where(core == 0, high, low)
        last_send[q] = jnp.concatenate([give[:, : width // 2], give[:, width // 2 :]], axis=0).astype(BF16)
        h_copies[q] = remote(last_send.at[q], last_recv.at[q], h_sem, (q,), to_twin)
        h_copies[q].start()
        out[:, pl.ds(pl.multiple_of(core * half + q * width, width), width)] = keep.astype(BF16)
    for q in range(CHUNKS):
        h_copies[q].wait_recv()
        got = last_recv[q].astype(F32)
        joined = jnp.concatenate([got[:count], got[count:]], axis=1)
        out[:, pl.ds(pl.multiple_of((1 - core) * half + q * width, width), width)] = joined.astype(BF16)

    sent = [a_rows, a_meta, *bm_copies]
    for copies in (b_copies, c_copies, d_copies, e_copies, f_copies, g_copies, h_copies):
        sent.extend(copies.values())
    for copy in sent:
        copy.wait_send()


def local(tokens, routes, route_weights, w_gate, w_up, w_down):
    groups, ranks = lax.axis_size("expert"), lax.axis_size("dp")
    count, features = tokens.shape
    units = w_gate.shape[2]
    capacity = 3 * count // groups
    block = -(-(ranks * capacity) // 16) * 16
    rows = groups * block
    half = features // 2
    width = half // CHUNKS
    chips = ranks // 2
    dma = pltpu.SemaphoreType.DMA
    return pl.pallas_call(
        functools.partial(kernel, groups, ranks, capacity, block),
        out_shape=jax.ShapeDtypeStruct((count, features), BF16),
        in_specs=[pl.BlockSpec(memory_space=pltpu.VMEM)] * 3 + [pl.BlockSpec(memory_space=pl.ANY)] * 3,
        out_specs=pl.BlockSpec(memory_space=pltpu.VMEM),
        scratch_shapes=[
            pltpu.VMEM((2 * CHUNKS, width, units), BF16),
            pltpu.VMEM((2 * CHUNKS, width, units), BF16),
            pltpu.VMEM((2 * CHUNKS, units, width), BF16),
            dma((3, CHUNKS, 2)),
            pltpu.VMEM((2 * count, half // 2), BF16),
            pltpu.VMEM((2 * count, half // 2), BF16),
            pltpu.VMEM((ranks * count, 128), F32),
            pltpu.VMEM((CHUNKS, ranks * count, width), BF16),
            pltpu.VMEM((CHUNKS, rows, width), BF16),
            pltpu.VMEM((2, CHUNKS, rows, width), BF16),
            pltpu.VMEM((rows, units), F32),
            pltpu.VMEM((rows, units), F32),
            pltpu.VMEM((rows, units), BF16),
            pltpu.VMEM((CHUNKS, rows, width), BF16),
            pltpu.VMEM((CHUNKS, rows, width), BF16),
            pltpu.VMEM((CHUNKS, rows, width), BF16),
            pltpu.VMEM((CHUNKS, rows, width), BF16),
            pltpu.VMEM((CHUNKS, ranks * count, width), BF16),
            pltpu.VMEM((CHUNKS, ranks * count, width), BF16),
            pltpu.VMEM((CHUNKS, 2 * count, width // 2), BF16),
            pltpu.VMEM((CHUNKS, 2 * count, width // 2), BF16),
            dma((2, 2)),
            dma((2, CHUNKS, chips - 1)),
            dma((2, chips - 1)),
            dma((2, CHUNKS, groups - 1)),
            dma((2, CHUNKS, groups)),
            dma((2, CHUNKS)),
            dma((2, CHUNKS, groups - 1)),
            dma((2, CHUNKS, chips - 1)),
            dma((2, CHUNKS)),
        ],
        compiler_params=pltpu.CompilerParams(
            collective_id=0, has_side_effects=True, vmem_limit_bytes=60 * 1024 * 1024
        ),
        cost_estimate=pl.CostEstimate(
            flops=6 * rows * features * units, bytes_accessed=6 * features * units, transcendentals=rows * units
        ),
    )(tokens, routes, route_weights, w_gate[0], w_up[0], w_down[0])


def solution(mesh):
    placed = (
        P(("expert", "dp"), None),
        P(("expert", "dp"), None),
        P(("expert", "dp"), None),
        P("expert", None, "dp"),
        P("expert", None, "dp"),
        P("expert", "dp", None),
    )
    return jax.shard_map(
        local, mesh=mesh, in_specs=placed, out_specs=P(("expert", "dp"), None), check_vma=False
    )
```

```python
import functools

import jax
import jax.numpy as jnp
from jax import lax
from jax.experimental import pallas as pl
from jax.experimental.pallas import tpu as pltpu
from jax.sharding import PartitionSpec as P

MESH = pl.DeviceIdType.MESH
BF16 = jnp.bfloat16
F32 = jnp.float32
CHUNKS = 4


def tile_of(extent, most):
    return max([t for t in range(128, most + 1, 128) if extent % t == 0], default=extent)


def kernel(
    groups, ranks, capacity, block,
    tokens, routes, weights, gate_hbm, up_hbm, down_hbm, out,
    gate, up, down, w_sem,
    folded, meta, gathered, chosen_rows, lhs, g_acc, u_acc, hidden,
    half_send, half_recv, summed, returned, mixed_send, mixed_recv,
    b_sem, bm_sem, c_sem, d_sem, e_sem, f_sem, g_sem,
):
    expert = lax.axis_index("expert")
    rank = lax.axis_index("dp")
    core = lax.rem(rank, 2)
    twin = rank + 1 - 2 * core
    count, features = tokens.shape
    units = gate_hbm.shape[1]
    half = features // 2
    width = half // CHUNKS
    fold = width // 2
    rows = groups * block
    both = 2 * count

    def rank_rows(r):
        return pl.ds(pl.multiple_of(r * both, both), both)

    def block_rows(e):
        return pl.ds(pl.multiple_of(e * block, block), block)

    def remote(src, dst, sems, index, where):
        return pltpu.make_async_remote_copy(
            src_ref=src, dst_ref=dst, send_sem=sems.at[(0, *index)], recv_sem=sems.at[(1, *index)],
            device_id=where, device_id_type=MESH,
        )

    to_twin = {"dp": twin}
    rank_peers = [(d, {"dp": lax.rem(rank + d, ranks)}, lax.rem(rank + d, ranks)) for d in range(1, ranks)]
    expert_peers = [(d, {"expert": lax.rem(expert + d, groups)}, lax.rem(expert + d, groups)) for d in range(1, groups)]

    barrier = pltpu.get_barrier_semaphore()
    for _, where, _ in rank_peers + expert_peers:
        pl.semaphore_signal(barrier, inc=1, device_id=where, device_id_type=MESH)

    loads = {}
    for q in range(CHUNKS):
        for side in range(2):
            at = (core if side == 0 else 1 - core) * CHUNKS + q
            span = pl.ds(pl.multiple_of(at * width, width), width)
            loads["in", q, side] = (
                pltpu.make_async_copy(gate_hbm.at[span, :], gate.at[at], w_sem.at[0, q, side]),
                pltpu.make_async_copy(up_hbm.at[span, :], up.at[at], w_sem.at[1, q, side]),
            )
            for copy in loads["in", q, side]:
                copy.start()
    for q in range(CHUNKS):
        for side in (1, 0):
            at = (core if side == 0 else 1 - core) * CHUNKS + q
            span = pl.ds(pl.multiple_of(at * width, width), width)
            loads["out", q, side] = pltpu.make_async_copy(down_hbm.at[:, span], down.at[at], w_sem.at[2, q, side])
            loads["out", q, side].start()

    for side in range(2):
        for q in range(CHUNKS):
            at = side * half + q * width
            piece = tokens[:, at : at + width].astype(F32)
            folded[side, q] = jnp.concatenate([piece[:, :fold], piece[:, fold:]], axis=0).astype(BF16)
    for q in range(CHUNKS):
        gathered[q, rank_rows(rank), :] = folded[core, q]

    diagonal = lax.broadcasted_iota(jnp.int32, (count, count), 0) == lax.broadcasted_iota(jnp.int32, (count, count), 1)

    def upright(line):
        return jnp.sum(jnp.where(diagonal, line, 0.0), axis=1, keepdims=True)

    first, second = upright(routes[0:1, :].astype(F32)), upright(routes[1:2, :].astype(F32))
    lanes = lax.broadcasted_iota(jnp.int32, (count, 128), 1)
    is_first = (lanes.astype(F32) == first).astype(F32)
    is_second = (lanes.astype(F32) == second).astype(F32)
    earlier = (
        lax.broadcasted_iota(jnp.int32, (count, count), 1) < lax.broadcasted_iota(jnp.int32, (count, count), 0)
    ).astype(F32)
    before = jnp.dot(earlier, is_first + is_second, preferred_element_type=F32)
    slot_first = jnp.sum(before * is_first, axis=1, keepdims=True)
    slot_second = jnp.sum((before + is_first) * is_second, axis=1, keepdims=True)
    base = (rank * capacity).astype(F32)
    row_first = first * block + base + slot_first
    row_second = second * block + base + slot_second
    facts = jnp.where(lanes == 2, upright(weights[0:1, :]), -1.0)
    facts = jnp.where(lanes == 3, upright(weights[1:2, :]), facts)
    upper = jnp.where(lanes == 0, row_first, jnp.where(lanes == 1, row_second, facts))
    lower = jnp.where(lanes == 4, row_first, jnp.where(lanes == 5, row_second, facts))
    meta[rank_rows(rank), :] = jnp.concatenate([upper, lower], axis=0)

    pl.semaphore_wait(barrier, len(rank_peers) + len(expert_peers))

    b_copies, bm_copies = {}, {}
    for d, where, there in rank_peers:
        part = meta.at[rank_rows(rank), :]
        bm_copies[d] = remote(part, part, bm_sem, (d - 1,), where)
        bm_copies[d].start()
    for q in range(CHUNKS):
        for d, where, there in rank_peers:
            b_copies[q, d] = remote(
                folded.at[lax.rem(there, 2), q], gathered.at[q, rank_rows(rank), :], b_sem, (q, d - 1), where
            )
            b_copies[q, d].start()
    for copy in bm_copies.values():
        copy.wait_recv()
    table = meta[...]
    turned = table.T
    row_ids = lax.broadcasted_iota(jnp.int32, (ranks * both, rows), 1).astype(F32)
    picks_left, picks_right = (
        jnp.concatenate([(row_ids == table[:, k : k + 1]).astype(BF16) for k in (n, n + 1)], axis=0) for n in (0, 4)
    )
    row_ids = lax.broadcasted_iota(jnp.int32, (rows, ranks * both), 0).astype(F32)
    place_left, place_right = (
        ((row_ids == turned[n : n + 1, :]).astype(F32) + (row_ids == turned[n + 1 : n + 2, :]).astype(F32)).astype(BF16)
        for n in (0, 4)
    )

    c_copies, d_copies = {}, {}
    for q in range(CHUNKS):
        for d, _, _ in rank_peers:
            b_copies[q, d].wait_recv()
        chosen_rows[q, :, :fold] = jnp.dot(place_left, gathered[q], preferred_element_type=F32).astype(BF16)
        chosen_rows[q, :, fold:] = jnp.dot(place_right, gathered[q], preferred_element_type=F32).astype(BF16)
        for d, where, there in expert_peers:
            c_copies[q, d] = remote(
                chosen_rows.at[q, block_rows(there), :], lhs.at[core, q, block_rows(expert), :],
                c_sem, (q, d - 1), where,
            )
            c_copies[q, d].start()
        lhs[core, q, block_rows(expert), :] = chosen_rows[q, block_rows(expert), :]
        part = lhs.at[core, q, block_rows(expert), :]
        d_copies[q, 0] = remote(part, part, d_sem, (q, 0), to_twin)
        d_copies[q, 0].start()

    unit_tile = tile_of(units, 512)

    def accumulate(q, side, fresh=False, last=False):
        at = core if side == 0 else 1 - core
        for copy in loads["in", q, side]:
            copy.wait()
        piece = at * CHUNKS + q

        def step(n, carry):
            span = pl.ds(pl.multiple_of(n * unit_tile, unit_tile), unit_tile)
            x = lhs[at, q]
            g = jnp.dot(x, gate[piece, :, span], preferred_element_type=F32)
            u = jnp.dot(x, up[piece, :, span], preferred_element_type=F32)
            if not fresh:
                g = g_acc[:, span] + g
                u = u_acc[:, span] + u
            if last:
                hidden[:, span] = (g / (1.0 + jnp.exp(-g)) * u).astype(BF16)
            else:
                g_acc[:, span] = g
                u_acc[:, span] = u
            return carry

        lax.fori_loop(0, units // unit_tile, step, 0)

    for q in range(CHUNKS):
        for d, _, _ in expert_peers:
            c_copies[q, d].wait_recv()
            part = lhs.at[core, q, block_rows(lax.rem(expert + groups - d, groups)), :]
            d_copies[q, d] = remote(part, part, d_sem, (q, d), to_twin)
            d_copies[q, d].start()
        accumulate(q, 0, fresh=q == 0)
        for d in range(groups):
            d_copies[q, d].wait_recv()
        accumulate(q, 1, last=q == CHUNKS - 1)

    out_tile = tile_of(width, 512)
    e_copies, f_copies = {}, {}

    def foreign(q):
        loads["out", q, 1].wait()

        def step(n, carry):
            span = pl.ds(pl.multiple_of(n * out_tile, out_tile), out_tile)
            half_send[q, :, span] = jnp.dot(
                hidden[...], down[(1 - core) * CHUNKS + q, :, span], preferred_element_type=F32
            ).astype(BF16)
            return carry

        lax.fori_loop(0, width // out_tile, step, 0)
        e_copies[q] = remote(half_send.at[q], half_recv.at[q], e_sem, (q,), to_twin)
        e_copies[q].start()

    def native(q):
        loads["out", q, 0].wait()
        e_copies[q].wait_recv()

        def step(n, carry):
            span = pl.ds(pl.multiple_of(n * out_tile, out_tile), out_tile)
            part = jnp.dot(hidden[...], down[core * CHUNKS + q, :, span], preferred_element_type=F32)
            summed[q, :, span] = (part + half_recv[q, :, span].astype(F32)).astype(BF16)
            return carry

        lax.fori_loop(0, width // out_tile, step, 0)
        for d, where, there in expert_peers:
            f_copies[q, d] = remote(
                summed.at[q, block_rows(there), :], returned.at[q, block_rows(expert), :], f_sem, (q, d - 1), where
            )
            f_copies[q, d].start()
        returned[q, block_rows(expert), :] = summed[q, block_rows(expert), :]

    foreign(0)
    for q in range(CHUNKS):
        if q + 1 < CHUNKS:
            foreign(q + 1)
        native(q)

    g_copies = {}
    folded_rows = ranks * both
    for q in range(CHUNKS):
        for d, _, _ in expert_peers:
            f_copies[q, d].wait_recv()
        picked = jnp.dot(picks_left, returned[q, :, :fold], preferred_element_type=F32) + jnp.dot(
            picks_right, returned[q, :, fold:], preferred_element_type=F32
        )
        mixture = table[:, 2:3] * picked[:folded_rows] + table[:, 3:4] * picked[folded_rows:]
        mixed_send[q] = mixture.astype(BF16)
        for d, where, there in rank_peers:
            g_copies[q, d] = remote(
                mixed_send.at[q, rank_rows(there), :], mixed_recv.at[q, rank_rows(rank), :], g_sem, (q, d - 1), where
            )
            g_copies[q, d].start()
        mixed_recv[q, rank_rows(rank), :] = mixed_send[q, rank_rows(rank), :]

    for q in range(CHUNKS):
        for d, _, _ in rank_peers:
            g_copies[q, d].wait_recv()
        for side in range(2):
            total = mixed_recv[q, side * both : (side + 1) * both, :].astype(F32)
            for r in range(side + 2, ranks, 2):
                total = total + mixed_recv[q, r * both : (r + 1) * both, :].astype(F32)
            at = side * half + q * width
            out[:, at : at + fold] = total[:count].astype(BF16)
            out[:, at + fold : at + width] = total[count:].astype(BF16)

    for copies in (bm_copies, b_copies, c_copies, d_copies, e_copies, f_copies, g_copies):
        for copy in copies.values():
            copy.wait_send()


def local(tokens, routes, route_weights, w_gate, w_up, w_down):
    groups, ranks = lax.axis_size("expert"), lax.axis_size("dp")
    count, features = tokens.shape
    units = w_gate.shape[2]
    capacity = 3 * count // groups
    block = -(-(ranks * capacity) // 16) * 16
    rows = groups * block
    half = features // 2
    width = half // CHUNKS
    both = 2 * count
    dma = pltpu.SemaphoreType.DMA
    return pl.pallas_call(
        functools.partial(kernel, groups, ranks, capacity, block),
        out_shape=jax.ShapeDtypeStruct((count, features), BF16),
        in_specs=[pl.BlockSpec(memory_space=pltpu.VMEM)] * 3 + [pl.BlockSpec(memory_space=pl.ANY)] * 3,
        out_specs=pl.BlockSpec(memory_space=pltpu.VMEM),
        scratch_shapes=[
            pltpu.VMEM((2 * CHUNKS, width, units), BF16),
            pltpu.VMEM((2 * CHUNKS, width, units), BF16),
            pltpu.VMEM((2 * CHUNKS, units, width), BF16),
            dma((3, CHUNKS, 2)),
            pltpu.VMEM((2, CHUNKS, both, width // 2), BF16),
            pltpu.VMEM((ranks * both, 128), F32),
            pltpu.VMEM((CHUNKS, ranks * both, width // 2), BF16),
            pltpu.VMEM((CHUNKS, rows, width), BF16),
            pltpu.VMEM((2, CHUNKS, rows, width), BF16),
            pltpu.VMEM((rows, units), F32),
            pltpu.VMEM((rows, units), F32),
            pltpu.VMEM((rows, units), BF16),
            pltpu.VMEM((CHUNKS, rows, width), BF16),
            pltpu.VMEM((CHUNKS, rows, width), BF16),
            pltpu.VMEM((CHUNKS, rows, width), BF16),
            pltpu.VMEM((CHUNKS, rows, width), BF16),
            pltpu.VMEM((CHUNKS, ranks * both, width // 2), BF16),
            pltpu.VMEM((CHUNKS, ranks * both, width // 2), BF16),
            dma((2, CHUNKS, ranks - 1)),
            dma((2, ranks - 1)),
            dma((2, CHUNKS, groups - 1)),
            dma((2, CHUNKS, groups)),
            dma((2, CHUNKS)),
            dma((2, CHUNKS, groups - 1)),
            dma((2, CHUNKS, ranks - 1)),
        ],
        compiler_params=pltpu.CompilerParams(
            collective_id=0, has_side_effects=True, vmem_limit_bytes=60 * 1024 * 1024
        ),
        cost_estimate=pl.CostEstimate(
            flops=6 * rows * features * units, bytes_accessed=6 * features * units, transcendentals=rows * units
        ),
    )(tokens, routes.T, route_weights.T, w_gate[0], w_up[0], w_down[0])


def solution(mesh):
    placed = (
        P(("expert", "dp"), None),
        P(("expert", "dp"), None),
        P(("expert", "dp"), None),
        P("expert", None, "dp"),
        P("expert", None, "dp"),
        P("expert", "dp", None),
    )
    return jax.shard_map(
        local, mesh=mesh, in_specs=placed, out_specs=P(("expert", "dp"), None), check_vma=False
    )
```

```python
import functools

import jax
import jax.numpy as jnp
from jax import lax
from jax.experimental import pallas as pl
from jax.experimental.pallas import tpu as pltpu
from jax.sharding import PartitionSpec as P

MESH = pl.DeviceIdType.MESH
BF16 = jnp.bfloat16
F32 = jnp.float32
CHUNKS = 4
TOKEN_GROUPS = ((0, 1), (1, 3))
RESULT_GROUPS = ((0, 2), (2, 1), (3, 1))


def tile_of(extent, most):
    return max([t for t in range(128, most + 1, 128) if extent % t == 0], default=extent)


def kernel(
    groups, ranks, capacity, block,
    tokens, routes, weights, gate_hbm, up_hbm, down_hbm, out,
    gate, up, down, w_sem,
    folded, meta, gathered, chosen_rows, lhs, g_acc, u_acc, hidden,
    half_send, half_recv, summed, returned, mixed_send, mixed_recv,
    b_sem, bm_sem, c_sem, d_sem, e_sem, f_sem, g_sem,
):
    expert = lax.axis_index("expert")
    rank = lax.axis_index("dp")
    core = lax.rem(rank, 2)
    twin = rank + 1 - 2 * core
    count, features = tokens.shape
    units = gate_hbm.shape[1]
    half = features // 2
    width = half // CHUNKS
    fold = width // 2
    rows = groups * block
    both = 2 * count

    def rank_rows(r):
        return pl.ds(pl.multiple_of(r * both, both), both)

    def block_rows(e):
        return pl.ds(pl.multiple_of(e * block, block), block)

    def remote(src, dst, sems, index, where):
        return pltpu.make_async_remote_copy(
            src_ref=src, dst_ref=dst, send_sem=sems.at[(0, *index)], recv_sem=sems.at[(1, *index)],
            device_id=where, device_id_type=MESH,
        )

    to_twin = {"dp": twin}
    rank_peers = [(d, {"dp": lax.rem(rank + d, ranks)}, lax.rem(rank + d, ranks)) for d in range(1, ranks)]
    expert_peers = [(d, {"expert": lax.rem(expert + d, groups)}, lax.rem(expert + d, groups)) for d in range(1, groups)]

    barrier = pltpu.get_barrier_semaphore()
    for _, where, _ in rank_peers + expert_peers:
        pl.semaphore_signal(barrier, inc=1, device_id=where, device_id_type=MESH)

    loads = {}
    for q in range(CHUNKS):
        for side in range(2):
            at = (core if side == 0 else 1 - core) * CHUNKS + q
            span = pl.ds(pl.multiple_of(at * width, width), width)
            loads["in", q, side] = (
                pltpu.make_async_copy(gate_hbm.at[span, :], gate.at[at], w_sem.at[0, q, side]),
                pltpu.make_async_copy(up_hbm.at[span, :], up.at[at], w_sem.at[1, q, side]),
            )
            for copy in loads["in", q, side]:
                copy.start()
    for q in range(CHUNKS):
        for side in (1, 0):
            at = (core if side == 0 else 1 - core) * CHUNKS + q
            span = pl.ds(pl.multiple_of(at * width, width), width)
            loads["out", q, side] = pltpu.make_async_copy(down_hbm.at[:, span], down.at[at], w_sem.at[2, q, side])
            loads["out", q, side].start()

    for side in range(2):
        for q in range(CHUNKS):
            at = side * half + q * width
            piece = tokens[:, at : at + width].astype(F32)
            folded[side, q] = jnp.concatenate([piece[:, :fold], piece[:, fold:]], axis=0).astype(BF16)
    for q in range(CHUNKS):
        gathered[q, rank_rows(rank), :] = folded[core, q]

    diagonal = lax.broadcasted_iota(jnp.int32, (count, count), 0) == lax.broadcasted_iota(jnp.int32, (count, count), 1)

    def upright(line):
        return jnp.sum(jnp.where(diagonal, line, 0.0), axis=1, keepdims=True)

    first, second = upright(routes[0:1, :].astype(F32)), upright(routes[1:2, :].astype(F32))
    lanes = lax.broadcasted_iota(jnp.int32, (count, 128), 1)
    is_first = (lanes.astype(F32) == first).astype(F32)
    is_second = (lanes.astype(F32) == second).astype(F32)
    earlier = (
        lax.broadcasted_iota(jnp.int32, (count, count), 1) < lax.broadcasted_iota(jnp.int32, (count, count), 0)
    ).astype(F32)
    before = jnp.dot(earlier, is_first + is_second, preferred_element_type=F32)
    slot_first = jnp.sum(before * is_first, axis=1, keepdims=True)
    slot_second = jnp.sum((before + is_first) * is_second, axis=1, keepdims=True)
    base = (rank * capacity).astype(F32)
    row_first = first * block + base + slot_first
    row_second = second * block + base + slot_second
    facts = jnp.where(lanes == 2, upright(weights[0:1, :]), -1.0)
    facts = jnp.where(lanes == 3, upright(weights[1:2, :]), facts)
    upper = jnp.where(lanes == 0, row_first, jnp.where(lanes == 1, row_second, facts))
    lower = jnp.where(lanes == 4, row_first, jnp.where(lanes == 5, row_second, facts))
    meta[rank_rows(rank), :] = jnp.concatenate([upper, lower], axis=0)

    pl.semaphore_wait(barrier, len(rank_peers) + len(expert_peers))

    b_copies, bm_copies = {}, {}
    for d, where, there in rank_peers:
        part = meta.at[rank_rows(rank), :]
        bm_copies[d] = remote(part, part, bm_sem, (d - 1,), where)
        bm_copies[d].start()
    for q, n in TOKEN_GROUPS:
        for d, where, there in rank_peers:
            b_copies[q, d] = remote(
                folded.at[lax.rem(there, 2), pl.ds(q, n)], gathered.at[pl.ds(q, n), rank_rows(rank), :],
                b_sem, (q, d - 1), where,
            )
            b_copies[q, d].start()
    for copy in bm_copies.values():
        copy.wait_recv()
    table = meta[...]
    turned = table.T
    row_ids = lax.broadcasted_iota(jnp.int32, (ranks * both, rows), 1).astype(F32)
    picks_left, picks_right = (
        jnp.concatenate([(row_ids == table[:, k : k + 1]).astype(BF16) for k in (n, n + 1)], axis=0) for n in (0, 4)
    )
    row_ids = lax.broadcasted_iota(jnp.int32, (rows, ranks * both), 0).astype(F32)
    place_left, place_right = (
        ((row_ids == turned[n : n + 1, :]).astype(F32) + (row_ids == turned[n + 1 : n + 2, :]).astype(F32)).astype(BF16)
        for n in (0, 4)
    )

    c_copies, d_copies = {}, {}
    for q in range(CHUNKS):
        for d, _, _ in rank_peers:
            if (q, d) in b_copies:
                b_copies[q, d].wait_recv()
        chosen_rows[q, :, :fold] = jnp.dot(place_left, gathered[q], preferred_element_type=F32).astype(BF16)
        chosen_rows[q, :, fold:] = jnp.dot(place_right, gathered[q], preferred_element_type=F32).astype(BF16)
        for d, where, there in expert_peers:
            c_copies[q, d] = remote(
                chosen_rows.at[q, block_rows(there), :], lhs.at[core, q, block_rows(expert), :],
                c_sem, (q, d - 1), where,
            )
            c_copies[q, d].start()
        lhs[core, q, block_rows(expert), :] = chosen_rows[q, block_rows(expert), :]
        part = lhs.at[core, q, block_rows(expert), :]
        d_copies[q, 0] = remote(part, part, d_sem, (q, 0), to_twin)
        d_copies[q, 0].start()

    unit_tile = tile_of(units, 256)

    def accumulate(q, side, fresh=False, last=False):
        at = core if side == 0 else 1 - core
        for copy in loads["in", q, side]:
            copy.wait()
        piece = at * CHUNKS + q

        def step(n, carry):
            span = pl.ds(pl.multiple_of(n * unit_tile, unit_tile), unit_tile)
            x = lhs[at, q]
            g = jnp.dot(x, gate[piece, :, span], preferred_element_type=F32)
            u = jnp.dot(x, up[piece, :, span], preferred_element_type=F32)
            if not fresh:
                g = g_acc[:, span] + g
                u = u_acc[:, span] + u
            if last:
                hidden[:, span] = (g / (1.0 + jnp.exp(-g)) * u).astype(BF16)
            else:
                g_acc[:, span] = g
                u_acc[:, span] = u
            return carry

        lax.fori_loop(0, units // unit_tile, step, 0, unroll=True)

    for q in range(CHUNKS):
        for d, _, _ in expert_peers:
            c_copies[q, d].wait_recv()
            part = lhs.at[core, q, block_rows(lax.rem(expert + groups - d, groups)), :]
            d_copies[q, d] = remote(part, part, d_sem, (q, d), to_twin)
            d_copies[q, d].start()
        accumulate(q, 0, fresh=q == 0)
        for d in range(groups):
            d_copies[q, d].wait_recv()
        accumulate(q, 1, last=q == CHUNKS - 1)

    out_tile = tile_of(width, 256)
    e_copies, f_copies = {}, {}

    def foreign(q):
        loads["out", q, 1].wait()

        def step(n, carry):
            span = pl.ds(pl.multiple_of(n * out_tile, out_tile), out_tile)
            half_send[q, :, span] = jnp.dot(
                hidden[...], down[(1 - core) * CHUNKS + q, :, span], preferred_element_type=F32
            ).astype(BF16)
            return carry

        lax.fori_loop(0, width // out_tile, step, 0, unroll=True)
        e_copies[q] = remote(half_send.at[q], half_recv.at[q], e_sem, (q,), to_twin)
        e_copies[q].start()

    def native(q):
        loads["out", q, 0].wait()
        e_copies[q].wait_recv()

        def step(n, carry):
            span = pl.ds(pl.multiple_of(n * out_tile, out_tile), out_tile)
            part = jnp.dot(hidden[...], down[core * CHUNKS + q, :, span], preferred_element_type=F32)
            summed[q, :, span] = (part + half_recv[q, :, span].astype(F32)).astype(BF16)
            return carry

        lax.fori_loop(0, width // out_tile, step, 0, unroll=True)
        for d, where, there in expert_peers:
            f_copies[q, d] = remote(
                summed.at[q, block_rows(there), :], returned.at[q, block_rows(expert), :], f_sem, (q, d - 1), where
            )
            f_copies[q, d].start()
        returned[q, block_rows(expert), :] = summed[q, block_rows(expert), :]

    foreign(0)
    for q in range(CHUNKS):
        if q + 1 < CHUNKS:
            foreign(q + 1)
        native(q)

    for copies in (bm_copies, b_copies, c_copies, d_copies, e_copies):
        for copy in copies.values():
            copy.wait_send()
    g_copies = {}
    folded_rows = ranks * both
    ready = {q + n - 1: (q, n) for q, n in RESULT_GROUPS}
    for q in range(CHUNKS):
        for d, _, _ in expert_peers:
            f_copies[q, d].wait_recv()
        picked = jnp.dot(picks_left, returned[q, :, :fold], preferred_element_type=F32) + jnp.dot(
            picks_right, returned[q, :, fold:], preferred_element_type=F32
        )
        mixture = table[:, 2:3] * picked[:folded_rows] + table[:, 3:4] * picked[folded_rows:]
        mixed_send[q] = mixture.astype(BF16)
        mixed_recv[q, rank_rows(rank), :] = mixed_send[q, rank_rows(rank), :]
        if q not in ready:
            continue
        at, n = ready[q]
        for d, where, there in rank_peers:
            g_copies[at, d] = remote(
                mixed_send.at[pl.ds(at, n), rank_rows(there), :], mixed_recv.at[pl.ds(at, n), rank_rows(rank), :],
                g_sem, (at, d - 1), where,
            )
            g_copies[at, d].start()

    for copy in f_copies.values():
        copy.wait_send()
    for q in range(CHUNKS):
        for d, _, _ in rank_peers:
            if (q, d) in g_copies:
                g_copies[q, d].wait_recv()
        for side in range(2):
            total = mixed_recv[q, side * both : (side + 1) * both, :].astype(F32)
            for r in range(side + 2, ranks, 2):
                total = total + mixed_recv[q, r * both : (r + 1) * both, :].astype(F32)
            at = side * half + q * width
            out[:, at : at + fold] = total[:count].astype(BF16)
            out[:, at + fold : at + width] = total[count:].astype(BF16)

    for copy in g_copies.values():
        copy.wait_send()


def local(tokens, routes, route_weights, w_gate, w_up, w_down):
    groups, ranks = lax.axis_size("expert"), lax.axis_size("dp")
    count, features = tokens.shape
    units = w_gate.shape[2]
    capacity = 3 * count // groups
    block = -(-(ranks * capacity) // 16) * 16
    rows = groups * block
    half = features // 2
    width = half // CHUNKS
    both = 2 * count
    dma = pltpu.SemaphoreType.DMA
    return pl.pallas_call(
        functools.partial(kernel, groups, ranks, capacity, block),
        out_shape=jax.ShapeDtypeStruct((count, features), BF16),
        in_specs=[pl.BlockSpec(memory_space=pltpu.VMEM)] * 3 + [pl.BlockSpec(memory_space=pl.ANY)] * 3,
        out_specs=pl.BlockSpec(memory_space=pltpu.VMEM),
        scratch_shapes=[
            pltpu.VMEM((2 * CHUNKS, width, units), BF16),
            pltpu.VMEM((2 * CHUNKS, width, units), BF16),
            pltpu.VMEM((2 * CHUNKS, units, width), BF16),
            dma((3, CHUNKS, 2)),
            pltpu.VMEM((2, CHUNKS, both, width // 2), BF16),
            pltpu.VMEM((ranks * both, 128), F32),
            pltpu.VMEM((CHUNKS, ranks * both, width // 2), BF16),
            pltpu.VMEM((CHUNKS, rows, width), BF16),
            pltpu.VMEM((2, CHUNKS, rows, width), BF16),
            pltpu.VMEM((rows, units), F32),
            pltpu.VMEM((rows, units), F32),
            pltpu.VMEM((rows, units), BF16),
            pltpu.VMEM((CHUNKS, rows, width), BF16),
            pltpu.VMEM((CHUNKS, rows, width), BF16),
            pltpu.VMEM((CHUNKS, rows, width), BF16),
            pltpu.VMEM((CHUNKS, rows, width), BF16),
            pltpu.VMEM((CHUNKS, ranks * both, width // 2), BF16),
            pltpu.VMEM((CHUNKS, ranks * both, width // 2), BF16),
            dma((2, CHUNKS, ranks - 1)),
            dma((2, ranks - 1)),
            dma((2, CHUNKS, groups - 1)),
            dma((2, CHUNKS, groups)),
            dma((2, CHUNKS)),
            dma((2, CHUNKS, groups - 1)),
            dma((2, CHUNKS, ranks - 1)),
        ],
        compiler_params=pltpu.CompilerParams(
            collective_id=0, has_side_effects=True, vmem_limit_bytes=60 * 1024 * 1024
        ),
        cost_estimate=pl.CostEstimate(
            flops=6 * rows * features * units, bytes_accessed=6 * features * units, transcendentals=rows * units
        ),
    )(tokens, routes.T, route_weights.T, w_gate[0], w_up[0], w_down[0])


def solution(mesh):
    placed = (
        P(("expert", "dp"), None),
        P(("expert", "dp"), None),
        P(("expert", "dp"), None),
        P("expert", None, "dp"),
        P("expert", None, "dp"),
        P("expert", "dp", None),
    )
    return jax.shard_map(
        local, mesh=mesh, in_specs=placed, out_specs=P(("expert", "dp"), None), check_vma=False
    )
```

```python
import functools

import jax
import jax.numpy as jnp
from jax import lax
from jax.experimental import pallas as pl
from jax.experimental.pallas import tpu as pltpu
from jax.sharding import PartitionSpec as P

MESH = pl.DeviceIdType.MESH
BF16 = jnp.bfloat16
F32 = jnp.float32
CHUNKS = 4
TOKEN_GROUPS = ((0, 1), (1, 3))
RESULT_GROUPS = ((0, 2), (2, 1), (3, 1))


def tiles_of(extent, most=512):
    return [slice(at, min(at + most, extent)) for at in range(0, extent, most)]


def kernel(
    groups, ranks, capacity, block,
    tokens, routes, weights, gate_hbm, up_hbm, down_hbm, out,
    gate, up, down, w_sem,
    folded, meta, gathered, chosen_rows, lhs, g_acc, u_acc, hidden,
    half_send, half_recv, summed, returned, mixed_send, mixed_recv,
    b_sem, bm_sem, c_sem, d_sem, e_sem, f_sem, g_sem,
):
    expert = lax.axis_index("expert")
    rank = lax.axis_index("dp")
    core = lax.rem(rank, 2)
    twin = rank + 1 - 2 * core
    count, features = tokens.shape
    units = gate_hbm.shape[1]
    half = features // 2
    width = half // CHUNKS
    fold = width // 2
    rows = groups * block
    both = 2 * count

    def rank_rows(r):
        return pl.ds(pl.multiple_of(r * both, both), both)

    def block_rows(e):
        return pl.ds(pl.multiple_of(e * block, block), block)

    def remote(src, dst, sems, index, where):
        return pltpu.make_async_remote_copy(
            src_ref=src, dst_ref=dst, send_sem=sems.at[(0, *index)], recv_sem=sems.at[(1, *index)],
            device_id=where, device_id_type=MESH,
        )

    to_twin = {"dp": twin}
    rank_peers = [(d, {"dp": lax.rem(rank + d, ranks)}, lax.rem(rank + d, ranks)) for d in range(1, ranks)]
    expert_peers = [(d, {"expert": lax.rem(expert + d, groups)}, lax.rem(expert + d, groups)) for d in range(1, groups)]

    barrier = pltpu.get_barrier_semaphore()
    for _, where, _ in rank_peers + expert_peers:
        pl.semaphore_signal(barrier, inc=1, device_id=where, device_id_type=MESH)

    loads = {}
    for q in range(CHUNKS):
        for side in range(2):
            at = (core if side == 0 else 1 - core) * CHUNKS + q
            span = pl.ds(pl.multiple_of(at * width, width), width)
            loads["in", q, side] = (
                pltpu.make_async_copy(gate_hbm.at[span, :], gate.at[at], w_sem.at[0, q, side]),
                pltpu.make_async_copy(up_hbm.at[span, :], up.at[at], w_sem.at[1, q, side]),
            )
            for copy in loads["in", q, side]:
                copy.start()
    for q in range(CHUNKS):
        for side in (1, 0):
            at = (core if side == 0 else 1 - core) * CHUNKS + q
            span = pl.ds(pl.multiple_of(at * width, width), width)
            loads["out", q, side] = pltpu.make_async_copy(down_hbm.at[:, span], down.at[at], w_sem.at[2, q, side])
            loads["out", q, side].start()

    for side in range(2):
        for q in range(CHUNKS):
            at = side * half + q * width
            piece = tokens[:, at : at + width].astype(F32)
            folded[side, q] = jnp.concatenate([piece[:, :fold], piece[:, fold:]], axis=0).astype(BF16)
    for q in range(CHUNKS):
        gathered[q, rank_rows(rank), :] = folded[core, q]

    diagonal = lax.broadcasted_iota(jnp.int32, (count, count), 0) == lax.broadcasted_iota(jnp.int32, (count, count), 1)

    def upright(line):
        return jnp.sum(jnp.where(diagonal, line, 0.0), axis=1, keepdims=True)

    first, second = upright(routes[0:1, :].astype(F32)), upright(routes[1:2, :].astype(F32))
    lanes = lax.broadcasted_iota(jnp.int32, (count, 128), 1)
    is_first = (lanes.astype(F32) == first).astype(F32)
    is_second = (lanes.astype(F32) == second).astype(F32)
    earlier = (
        lax.broadcasted_iota(jnp.int32, (count, count), 1) < lax.broadcasted_iota(jnp.int32, (count, count), 0)
    ).astype(F32)
    before = jnp.dot(earlier, is_first + is_second, preferred_element_type=F32)
    slot_first = jnp.sum(before * is_first, axis=1, keepdims=True)
    slot_second = jnp.sum((before + is_first) * is_second, axis=1, keepdims=True)
    base = (rank * capacity).astype(F32)
    row_first = first * block + base + slot_first
    row_second = second * block + base + slot_second
    facts = jnp.where(lanes == 2, upright(weights[0:1, :]), -1.0)
    facts = jnp.where(lanes == 3, upright(weights[1:2, :]), facts)
    upper = jnp.where(lanes == 0, row_first, jnp.where(lanes == 1, row_second, facts))
    lower = jnp.where(lanes == 4, row_first, jnp.where(lanes == 5, row_second, facts))
    meta[rank_rows(rank), :] = jnp.concatenate([upper, lower], axis=0)

    pl.semaphore_wait(barrier, len(rank_peers) + len(expert_peers))

    b_copies, bm_copies = {}, {}
    for d, where, there in rank_peers:
        part = meta.at[rank_rows(rank), :]
        bm_copies[d] = remote(part, part, bm_sem, (d - 1,), where)
        bm_copies[d].start()
    for q, n in TOKEN_GROUPS:
        for d, where, there in rank_peers:
            b_copies[q, d] = remote(
                folded.at[lax.rem(there, 2), pl.ds(q, n)], gathered.at[pl.ds(q, n), rank_rows(rank), :],
                b_sem, (q, d - 1), where,
            )
            b_copies[q, d].start()
    for copy in bm_copies.values():
        copy.wait_recv()
    table = meta[...]
    turned = table.T
    row_ids = lax.broadcasted_iota(jnp.int32, (ranks * both, rows), 1).astype(F32)
    picks_left, picks_right = (
        jnp.concatenate([(row_ids == table[:, k : k + 1]).astype(BF16) for k in (n, n + 1)], axis=0) for n in (0, 4)
    )
    row_ids = lax.broadcasted_iota(jnp.int32, (rows, ranks * both), 0).astype(F32)
    place_left, place_right = (
        ((row_ids == turned[n : n + 1, :]).astype(F32) + (row_ids == turned[n + 1 : n + 2, :]).astype(F32)).astype(BF16)
        for n in (0, 4)
    )

    c_copies, d_copies = {}, {}
    for q in range(CHUNKS):
        for d, _, _ in rank_peers:
            if (q, d) in b_copies:
                b_copies[q, d].wait_recv()
        chosen_rows[q, :, :fold] = jnp.dot(place_left, gathered[q], preferred_element_type=F32).astype(BF16)
        chosen_rows[q, :, fold:] = jnp.dot(place_right, gathered[q], preferred_element_type=F32).astype(BF16)
        for d, where, there in expert_peers:
            c_copies[q, d] = remote(
                chosen_rows.at[q, block_rows(there), :], lhs.at[core, q, block_rows(expert), :],
                c_sem, (q, d - 1), where,
            )
            c_copies[q, d].start()
        lhs[core, q, block_rows(expert), :] = chosen_rows[q, block_rows(expert), :]
        part = lhs.at[core, q, block_rows(expert), :]
        d_copies[q, 0] = remote(part, part, d_sem, (q, 0), to_twin)
        d_copies[q, 0].start()

    def accumulate(q, side, fresh=False, last=False):
        at = core if side == 0 else 1 - core
        for copy in loads["in", q, side]:
            copy.wait()
        piece = at * CHUNKS + q

        for span in tiles_of(units):
            x = lhs[at, q]
            g = jnp.dot(x, gate[piece, :, span], preferred_element_type=F32)
            u = jnp.dot(x, up[piece, :, span], preferred_element_type=F32)
            if not fresh:
                g = g_acc[:, span] + g
                u = u_acc[:, span] + u
            if last:
                hidden[:, span] = (g / (1.0 + jnp.exp(-g)) * u).astype(BF16)
            else:
                g_acc[:, span] = g
                u_acc[:, span] = u

    for q in range(CHUNKS):
        for d, _, _ in expert_peers:
            c_copies[q, d].wait_recv()
            part = lhs.at[core, q, block_rows(lax.rem(expert + groups - d, groups)), :]
            d_copies[q, d] = remote(part, part, d_sem, (q, d), to_twin)
            d_copies[q, d].start()
        accumulate(q, 0, fresh=q == 0)
        for d in range(groups):
            d_copies[q, d].wait_recv()
        accumulate(q, 1, last=q == CHUNKS - 1)

    e_copies, f_copies = {}, {}

    def foreign(q):
        loads["out", q, 1].wait()
        piece = (1 - core) * CHUNKS + q
        for span in tiles_of(width):
            half_send[q, :, span] = jnp.dot(
                hidden[...], down[piece, :, span], preferred_element_type=F32
            ).astype(BF16)
        e_copies[q] = remote(half_send.at[q], half_recv.at[q], e_sem, (q,), to_twin)
        e_copies[q].start()

    def native(q):
        loads["out", q, 0].wait()
        piece = core * CHUNKS + q
        parts = [jnp.dot(hidden[...], down[piece, :, span], preferred_element_type=F32) for span in tiles_of(width)]
        e_copies[q].wait_recv()
        for part, span in zip(parts, tiles_of(width)):
            summed[q, :, span] = (part + half_recv[q, :, span].astype(F32)).astype(BF16)
        for d, where, there in expert_peers:
            f_copies[q, d] = remote(
                summed.at[q, block_rows(there), :], returned.at[q, block_rows(expert), :], f_sem, (q, d - 1), where
            )
            f_copies[q, d].start()
        returned[q, block_rows(expert), :] = summed[q, block_rows(expert), :]

    foreign(0)
    native(0)
    foreign(1)
    for q in range(1, CHUNKS):
        if q + 1 < CHUNKS:
            foreign(q + 1)
        native(q)

    for copies in (bm_copies, b_copies, c_copies, d_copies, e_copies):
        for copy in copies.values():
            copy.wait_send()
    g_copies = {}
    folded_rows = ranks * both
    ready = {q + n - 1: (q, n) for q, n in RESULT_GROUPS}
    for q in range(CHUNKS):
        for d, _, _ in expert_peers:
            f_copies[q, d].wait_recv()
        picked = jnp.dot(picks_left, returned[q, :, :fold], preferred_element_type=F32) + jnp.dot(
            picks_right, returned[q, :, fold:], preferred_element_type=F32
        )
        mixture = table[:, 2:3] * picked[:folded_rows] + table[:, 3:4] * picked[folded_rows:]
        mixed_send[q] = mixture.astype(BF16)
        mixed_recv[q, rank_rows(rank), :] = mixed_send[q, rank_rows(rank), :]
        if q not in ready:
            continue
        at, n = ready[q]
        for d, where, there in rank_peers:
            g_copies[at, d] = remote(
                mixed_send.at[pl.ds(at, n), rank_rows(there), :], mixed_recv.at[pl.ds(at, n), rank_rows(rank), :],
                g_sem, (at, d - 1), where,
            )
            g_copies[at, d].start()

    for copy in f_copies.values():
        copy.wait_send()
    for q in range(CHUNKS):
        for d, _, _ in rank_peers:
            if (q, d) in g_copies:
                g_copies[q, d].wait_recv()
        for side in range(2):
            total = mixed_recv[q, side * both : (side + 1) * both, :].astype(F32)
            for r in range(side + 2, ranks, 2):
                total = total + mixed_recv[q, r * both : (r + 1) * both, :].astype(F32)
            at = side * half + q * width
            out[:, at : at + fold] = total[:count].astype(BF16)
            out[:, at + fold : at + width] = total[count:].astype(BF16)

    for copy in g_copies.values():
        copy.wait_send()


def local(tokens, routes, route_weights, w_gate, w_up, w_down):
    groups, ranks = lax.axis_size("expert"), lax.axis_size("dp")
    count, features = tokens.shape
    units = w_gate.shape[2]
    capacity = 3 * count // groups
    block = -(-(ranks * capacity) // 16) * 16
    rows = groups * block
    half = features // 2
    width = half // CHUNKS
    both = 2 * count
    dma = pltpu.SemaphoreType.DMA
    return pl.pallas_call(
        functools.partial(kernel, groups, ranks, capacity, block),
        out_shape=jax.ShapeDtypeStruct((count, features), BF16),
        in_specs=[pl.BlockSpec(memory_space=pltpu.VMEM)] * 3 + [pl.BlockSpec(memory_space=pl.ANY)] * 3,
        out_specs=pl.BlockSpec(memory_space=pltpu.VMEM),
        scratch_shapes=[
            pltpu.VMEM((2 * CHUNKS, width, units), BF16),
            pltpu.VMEM((2 * CHUNKS, width, units), BF16),
            pltpu.VMEM((2 * CHUNKS, units, width), BF16),
            dma((3, CHUNKS, 2)),
            pltpu.VMEM((2, CHUNKS, both, width // 2), BF16),
            pltpu.VMEM((ranks * both, 128), F32),
            pltpu.VMEM((CHUNKS, ranks * both, width // 2), BF16),
            pltpu.VMEM((CHUNKS, rows, width), BF16),
            pltpu.VMEM((2, CHUNKS, rows, width), BF16),
            pltpu.VMEM((rows, units), F32),
            pltpu.VMEM((rows, units), F32),
            pltpu.VMEM((rows, units), BF16),
            pltpu.VMEM((CHUNKS, rows, width), BF16),
            pltpu.VMEM((CHUNKS, rows, width), BF16),
            pltpu.VMEM((CHUNKS, rows, width), BF16),
            pltpu.VMEM((CHUNKS, rows, width), BF16),
            pltpu.VMEM((CHUNKS, ranks * both, width // 2), BF16),
            pltpu.VMEM((CHUNKS, ranks * both, width // 2), BF16),
            dma((2, CHUNKS, ranks - 1)),
            dma((2, ranks - 1)),
            dma((2, CHUNKS, groups - 1)),
            dma((2, CHUNKS, groups)),
            dma((2, CHUNKS)),
            dma((2, CHUNKS, groups - 1)),
            dma((2, CHUNKS, ranks - 1)),
        ],
        compiler_params=pltpu.CompilerParams(
            collective_id=0, has_side_effects=True, vmem_limit_bytes=60 * 1024 * 1024
        ),
        cost_estimate=pl.CostEstimate(
            flops=6 * rows * features * units, bytes_accessed=6 * features * units, transcendentals=rows * units
        ),
    )(tokens, routes.T, route_weights.T, w_gate[0], w_up[0], w_down[0])


def solution(mesh):
    placed = (
        P(("expert", "dp"), None),
        P(("expert", "dp"), None),
        P(("expert", "dp"), None),
        P("expert", None, "dp"),
        P("expert", None, "dp"),
        P("expert", "dp", None),
    )
    return jax.shard_map(
        local, mesh=mesh, in_specs=placed, out_specs=P(("expert", "dp"), None), check_vma=False
    )
```

```python
import functools

import jax
import jax.numpy as jnp
from jax import lax
from jax.experimental import pallas as pl
from jax.experimental.pallas import tpu as pltpu
from jax.sharding import PartitionSpec as P

MESH = pl.DeviceIdType.MESH
BF16 = jnp.bfloat16
F32 = jnp.float32
CHUNKS = 4
TOKEN_GROUPS = ((0, 1), (1, 3))
RESULT_GROUPS = ((0, 2), (2, 1), (3, 1))


def tile_of(extent, most):
    return max([t for t in range(128, most + 1, 128) if extent % t == 0], default=extent)


def kernel(
    groups, ranks, capacity, block,
    tokens, routes, weights, gate_hbm, up_hbm, down_hbm, out,
    gate, up, down, w_sem,
    folded, meta, gathered, chosen_rows, lhs, g_acc, u_acc, hidden,
    half_send, half_recv, summed, returned, mixed_send, mixed_recv,
    b_sem, bm_sem, c_sem, d_sem, e_sem, f_sem, g_sem,
):
    expert = lax.axis_index("expert")
    rank = lax.axis_index("dp")
    core = lax.rem(rank, 2)
    twin = rank + 1 - 2 * core
    count, features = tokens.shape
    units = gate_hbm.shape[1]
    half = features // 2
    width = half // CHUNKS
    fold = width // 2
    rows = groups * block
    both = 2 * count

    def rank_rows(r):
        return pl.ds(pl.multiple_of(r * both, both), both)

    def block_rows(e):
        return pl.ds(pl.multiple_of(e * block, block), block)

    def remote(src, dst, sems, index, where):
        return pltpu.make_async_remote_copy(
            src_ref=src, dst_ref=dst, send_sem=sems.at[(0, *index)], recv_sem=sems.at[(1, *index)],
            device_id=where, device_id_type=MESH,
        )

    to_twin = {"dp": twin}
    rank_peers = [(d, {"dp": lax.rem(rank + d, ranks)}, lax.rem(rank + d, ranks)) for d in range(1, ranks)]
    expert_peers = [(d, {"expert": lax.rem(expert + d, groups)}, lax.rem(expert + d, groups)) for d in range(1, groups)]

    barrier = pltpu.get_barrier_semaphore()
    for _, where, _ in rank_peers + expert_peers:
        pl.semaphore_signal(barrier, inc=1, device_id=where, device_id_type=MESH)

    loads = {}

    def load_in(q):
        for side in range(2):
            at = (core if side == 0 else 1 - core) * CHUNKS + q
            span = pl.ds(pl.multiple_of(at * width, width), width)
            loads["in", q, side] = (
                pltpu.make_async_copy(gate_hbm.at[span, :], gate.at[at], w_sem.at[0, q, side]),
                pltpu.make_async_copy(up_hbm.at[span, :], up.at[at], w_sem.at[1, q, side]),
            )
            for copy in loads["in", q, side]:
                copy.start()

    def load_out(q):
        for side in (1, 0):
            at = (core if side == 0 else 1 - core) * CHUNKS + q
            span = pl.ds(pl.multiple_of(at * width, width), width)
            loads["out", q, side] = pltpu.make_async_copy(down_hbm.at[:, span], down.at[at], w_sem.at[2, q, side])
            loads["out", q, side].start()

    load_in(0)

    for side in range(2):
        for q in range(CHUNKS):
            at = side * half + q * width
            piece = tokens[:, at : at + width].astype(F32)
            folded[side, q] = jnp.concatenate([piece[:, :fold], piece[:, fold:]], axis=0).astype(BF16)
    for q in range(CHUNKS):
        gathered[q, rank_rows(rank), :] = folded[core, q]

    diagonal = lax.broadcasted_iota(jnp.int32, (count, count), 0) == lax.broadcasted_iota(jnp.int32, (count, count), 1)

    def upright(line):
        return jnp.sum(jnp.where(diagonal, line, 0.0), axis=1, keepdims=True)

    first, second = upright(routes[0:1, :].astype(F32)), upright(routes[1:2, :].astype(F32))
    lanes = lax.broadcasted_iota(jnp.int32, (count, 128), 1)
    is_first = (lanes.astype(F32) == first).astype(F32)
    is_second = (lanes.astype(F32) == second).astype(F32)
    earlier = (
        lax.broadcasted_iota(jnp.int32, (count, count), 1) < lax.broadcasted_iota(jnp.int32, (count, count), 0)
    ).astype(F32)
    before = jnp.dot(earlier, is_first + is_second, preferred_element_type=F32)
    slot_first = jnp.sum(before * is_first, axis=1, keepdims=True)
    slot_second = jnp.sum((before + is_first) * is_second, axis=1, keepdims=True)
    base = (rank * capacity).astype(F32)
    row_first = first * block + base + slot_first
    row_second = second * block + base + slot_second
    facts = jnp.where(lanes == 2, upright(weights[0:1, :]), -1.0)
    facts = jnp.where(lanes == 3, upright(weights[1:2, :]), facts)
    upper = jnp.where(lanes == 0, row_first, jnp.where(lanes == 1, row_second, facts))
    lower = jnp.where(lanes == 4, row_first, jnp.where(lanes == 5, row_second, facts))
    meta[rank_rows(rank), :] = jnp.concatenate([upper, lower], axis=0)

    pl.semaphore_wait(barrier, len(rank_peers) + len(expert_peers))

    b_copies, bm_copies = {}, {}
    for d, where, there in rank_peers:
        part = meta.at[rank_rows(rank), :]
        bm_copies[d] = remote(part, part, bm_sem, (d - 1,), where)
        bm_copies[d].start()
    for q, n in TOKEN_GROUPS:
        for d, where, there in rank_peers:
            b_copies[q, d] = remote(
                folded.at[lax.rem(there, 2), pl.ds(q, n)], gathered.at[pl.ds(q, n), rank_rows(rank), :],
                b_sem, (q, d - 1), where,
            )
            b_copies[q, d].start()
    load_in(1)
    for copy in bm_copies.values():
        copy.wait_recv()
    table = meta[...]
    turned = table.T
    row_ids = lax.broadcasted_iota(jnp.int32, (ranks * both, rows), 1).astype(F32)
    picks_left, picks_right = (
        jnp.concatenate([(row_ids == table[:, k : k + 1]).astype(BF16) for k in (n, n + 1)], axis=0) for n in (0, 4)
    )
    row_ids = lax.broadcasted_iota(jnp.int32, (rows, ranks * both), 0).astype(F32)
    place_left, place_right = (
        ((row_ids == turned[n : n + 1, :]).astype(F32) + (row_ids == turned[n + 1 : n + 2, :]).astype(F32)).astype(BF16)
        for n in (0, 4)
    )

    c_copies, d_copies = {}, {}
    for q in range(CHUNKS):
        for d, _, _ in rank_peers:
            if (q, d) in b_copies:
                b_copies[q, d].wait_recv()
        chosen_rows[q, :, :fold] = jnp.dot(place_left, gathered[q], preferred_element_type=F32).astype(BF16)
        chosen_rows[q, :, fold:] = jnp.dot(place_right, gathered[q], preferred_element_type=F32).astype(BF16)
        for d, where, there in expert_peers:
            c_copies[q, d] = remote(
                chosen_rows.at[q, block_rows(there), :], lhs.at[core, q, block_rows(expert), :],
                c_sem, (q, d - 1), where,
            )
            c_copies[q, d].start()
        lhs[core, q, block_rows(expert), :] = chosen_rows[q, block_rows(expert), :]
        part = lhs.at[core, q, block_rows(expert), :]
        d_copies[q, 0] = remote(part, part, d_sem, (q, 0), to_twin)
        d_copies[q, 0].start()
        if q == 0:
            load_in(2)
    for q in range(3, CHUNKS):
        load_in(q)

    unit_tile = tile_of(units, 256)

    def accumulate(q, side, fresh=False, last=False):
        at = core if side == 0 else 1 - core
        for copy in loads["in", q, side]:
            copy.wait()
        piece = at * CHUNKS + q

        def step(n, carry):
            span = pl.ds(pl.multiple_of(n * unit_tile, unit_tile), unit_tile)
            x = lhs[at, q]
            g = jnp.dot(x, gate[piece, :, span], preferred_element_type=F32)
            u = jnp.dot(x, up[piece, :, span], preferred_element_type=F32)
            if not fresh:
                g = g_acc[:, span] + g
                u = u_acc[:, span] + u
            if last:
                hidden[:, span] = (g / (1.0 + jnp.exp(-g)) * u).astype(BF16)
            else:
                g_acc[:, span] = g
                u_acc[:, span] = u
            return carry

        lax.fori_loop(0, units // unit_tile, step, 0, unroll=True)

    for q in range(CHUNKS):
        for d, _, _ in expert_peers:
            c_copies[q, d].wait_recv()
            part = lhs.at[core, q, block_rows(lax.rem(expert + groups - d, groups)), :]
            d_copies[q, d] = remote(part, part, d_sem, (q, d), to_twin)
            d_copies[q, d].start()
        load_out(q)
        accumulate(q, 0, fresh=q == 0)
        for d in range(groups):
            d_copies[q, d].wait_recv()
        accumulate(q, 1, last=q == CHUNKS - 1)

    out_tile = tile_of(width, 256)
    e_copies, f_copies = {}, {}

    def foreign(q):
        loads["out", q, 1].wait()

        def step(n, carry):
            span = pl.ds(pl.multiple_of(n * out_tile, out_tile), out_tile)
            half_send[q, :, span] = jnp.dot(
                hidden[...], down[(1 - core) * CHUNKS + q, :, span], preferred_element_type=F32
            ).astype(BF16)
            return carry

        lax.fori_loop(0, width // out_tile, step, 0, unroll=True)
        e_copies[q] = remote(half_send.at[q], half_recv.at[q], e_sem, (q,), to_twin)
        e_copies[q].start()

    def native(q):
        loads["out", q, 0].wait()
        e_copies[q].wait_recv()

        def step(n, carry):
            span = pl.ds(pl.multiple_of(n * out_tile, out_tile), out_tile)
            part = jnp.dot(hidden[...], down[core * CHUNKS + q, :, span], preferred_element_type=F32)
            summed[q, :, span] = (part + half_recv[q, :, span].astype(F32)).astype(BF16)
            return carry

        lax.fori_loop(0, width // out_tile, step, 0, unroll=True)
        for d, where, there in expert_peers:
            f_copies[q, d] = remote(
                summed.at[q, block_rows(there), :], returned.at[q, block_rows(expert), :], f_sem, (q, d - 1), where
            )
            f_copies[q, d].start()
        returned[q, block_rows(expert), :] = summed[q, block_rows(expert), :]

    foreign(0)
    for q in range(CHUNKS):
        if q + 1 < CHUNKS:
            foreign(q + 1)
        native(q)

    for copies in (bm_copies, b_copies, c_copies, d_copies, e_copies):
        for copy in copies.values():
            copy.wait_send()
    g_copies = {}
    folded_rows = ranks * both
    ready = {q + n - 1: (q, n) for q, n in RESULT_GROUPS}
    for q in range(CHUNKS):
        for d, _, _ in expert_peers:
            f_copies[q, d].wait_recv()
        picked = jnp.dot(picks_left, returned[q, :, :fold], preferred_element_type=F32) + jnp.dot(
            picks_right, returned[q, :, fold:], preferred_element_type=F32
        )
        mixture = table[:, 2:3] * picked[:folded_rows] + table[:, 3:4] * picked[folded_rows:]
        mixed_send[q] = mixture.astype(BF16)
        mixed_recv[q, rank_rows(rank), :] = mixed_send[q, rank_rows(rank), :]
        if q not in ready:
            continue
        at, n = ready[q]
        for d, where, there in rank_peers:
            g_copies[at, d] = remote(
                mixed_send.at[pl.ds(at, n), rank_rows(there), :], mixed_recv.at[pl.ds(at, n), rank_rows(rank), :],
                g_sem, (at, d - 1), where,
            )
            g_copies[at, d].start()

    for copy in f_copies.values():
        copy.wait_send()
    for q in range(CHUNKS):
        for d, _, _ in rank_peers:
            if (q, d) in g_copies:
                g_copies[q, d].wait_recv()
        for side in range(2):
            total = mixed_recv[q, side * both : (side + 1) * both, :].astype(F32)
            for r in range(side + 2, ranks, 2):
                total = total + mixed_recv[q, r * both : (r + 1) * both, :].astype(F32)
            at = side * half + q * width
            out[:, at : at + fold] = total[:count].astype(BF16)
            out[:, at + fold : at + width] = total[count:].astype(BF16)

    for copy in g_copies.values():
        copy.wait_send()


def local(tokens, routes, route_weights, w_gate, w_up, w_down):
    groups, ranks = lax.axis_size("expert"), lax.axis_size("dp")
    count, features = tokens.shape
    units = w_gate.shape[2]
    capacity = 3 * count // groups
    block = -(-(ranks * capacity) // 16) * 16
    rows = groups * block
    half = features // 2
    width = half // CHUNKS
    both = 2 * count
    dma = pltpu.SemaphoreType.DMA
    return pl.pallas_call(
        functools.partial(kernel, groups, ranks, capacity, block),
        out_shape=jax.ShapeDtypeStruct((count, features), BF16),
        in_specs=[pl.BlockSpec(memory_space=pltpu.VMEM)] * 3 + [pl.BlockSpec(memory_space=pl.ANY)] * 3,
        out_specs=pl.BlockSpec(memory_space=pltpu.VMEM),
        scratch_shapes=[
            pltpu.VMEM((2 * CHUNKS, width, units), BF16),
            pltpu.VMEM((2 * CHUNKS, width, units), BF16),
            pltpu.VMEM((2 * CHUNKS, units, width), BF16),
            dma((3, CHUNKS, 2)),
            pltpu.VMEM((2, CHUNKS, both, width // 2), BF16),
            pltpu.VMEM((ranks * both, 128), F32),
            pltpu.VMEM((CHUNKS, ranks * both, width // 2), BF16),
            pltpu.VMEM((CHUNKS, rows, width), BF16),
            pltpu.VMEM((2, CHUNKS, rows, width), BF16),
            pltpu.VMEM((rows, units), F32),
            pltpu.VMEM((rows, units), F32),
            pltpu.VMEM((rows, units), BF16),
            pltpu.VMEM((CHUNKS, rows, width), BF16),
            pltpu.VMEM((CHUNKS, rows, width), BF16),
            pltpu.VMEM((CHUNKS, rows, width), BF16),
            pltpu.VMEM((CHUNKS, rows, width), BF16),
            pltpu.VMEM((CHUNKS, ranks * both, width // 2), BF16),
            pltpu.VMEM((CHUNKS, ranks * both, width // 2), BF16),
            dma((2, CHUNKS, ranks - 1)),
            dma((2, ranks - 1)),
            dma((2, CHUNKS, groups - 1)),
            dma((2, CHUNKS, groups)),
            dma((2, CHUNKS)),
            dma((2, CHUNKS, groups - 1)),
            dma((2, CHUNKS, ranks - 1)),
        ],
        compiler_params=pltpu.CompilerParams(
            collective_id=0, has_side_effects=True, vmem_limit_bytes=60 * 1024 * 1024
        ),
        cost_estimate=pl.CostEstimate(
            flops=6 * rows * features * units, bytes_accessed=6 * features * units, transcendentals=rows * units
        ),
    )(tokens, routes.T, route_weights.T, w_gate[0], w_up[0], w_down[0])


def solution(mesh):
    placed = (
        P(("expert", "dp"), None),
        P(("expert", "dp"), None),
        P(("expert", "dp"), None),
        P("expert", None, "dp"),
        P("expert", None, "dp"),
        P("expert", "dp", None),
    )
    return jax.shard_map(
        local, mesh=mesh, in_specs=placed, out_specs=P(("expert", "dp"), None), check_vma=False
    )
```
